512 devices in a mesh: prow: 16 (over z, core), pcol: 32 (over y, x).
Axes of the slice: x: 4, y: 8, z: 8, core: 2. Of those that a mesh axis runs over, the one named last changes fastest.
Arguments:
- right_side: float32 [3, 16, 32, 64, 256], P(None, 'prow', 'pcol'), may hold values from -6 to 6
- live_width: int32 [3, 16, 32], P(None, 'prow', 'pcol'), may hold values from 64 to 256
- lower_inverse: bfloat16 [3, 16, 32, 256, 256], P(None, 'prow', 'pcol'), as said below
- upper_inverse: bfloat16 [3, 16, 32, 256, 256], P(None, 'prow', 'pcol'), as said below
- lower_blocks: bfloat16 [3, 16, 32, 4, 256, 256], P(None, 'prow', 'pcol'), may hold values from -0.109375 to 0.109375
- lower_source: int32 [3, 16, 32, 4], P(None, 'prow', 'pcol'), may hold values from 0 to 31
- lower_target: int32 [3, 16, 32, 4], P(None, 'prow', 'pcol'), may hold values from 0 to 15
- upper_blocks: bfloat16 [3, 16, 32, 4, 256, 256], P(None, 'prow', 'pcol'), may hold values from -0.109375 to 0.109375
- upper_source: int32 [3, 16, 32, 4], P(None, 'prow', 'pcol'), may hold values from 0 to 31
- upper_target: int32 [3, 16, 32, 4], P(None, 'prow', 'pcol'), may hold values from 0 to 15
Outputs:
- forward_solution: float32 [3, 16, 32, 64, 256], P(None, 'prow', 'pcol')
- solution: float32 [3, 16, 32, 64, 256], P(None, 'prow', 'pcol')
The draws below stay inside these ranges and needn't reach their ends.
Inputs may be any that keep to these rules, and one draw needn't show every extreme that they name: lower_inverse[v, a, b] is upper triangular with unit diagonal. upper_inverse[v, a, b] is lower triangular with a positive diagonal.
All inputs are finite; a program needn't handle non-finite values.
Results may differ from the reference program's by a relative error of at most 0.023.
Values may be sent and summed in bfloat16 or wider, within the bound.
A program may use at most 64 MiB of HBM per device.

```python
import math
import jax
import jax.numpy as jnp
import numpy as np
from jax import lax

W = 256
R = 64
LEVELS = 3
CAP = 4
PAIRS = 3
N_PROW = 16
N_PCOL = 32


def triangle_parts(key, shape):
    noise = jax.random.normal(key, shape, jnp.float32)
    rows = lax.broadcasted_iota(jnp.int32, shape, 3)
    cols = lax.broadcasted_iota(jnp.int32, shape, 4)
    return (noise * (0.7 / math.sqrt(W)), rows, cols)


def draw_lower_inverse(key, part):
    key = jax.random.fold_in(key, 11)
    shape = (LEVELS, N_PROW, N_PCOL, W, W)
    values, rows, cols = triangle_parts(key, shape)
    above = jnp.where(cols > rows, values, 0.0)
    return (above + jnp.where(cols == rows, 1.0, 0.0)).astype(jnp.bfloat16)


def draw_upper_inverse(key, part):
    key = jax.random.fold_in(key, 23)
    first, second = jax.random.split(key)
    shape = (LEVELS, N_PROW, N_PCOL, W, W)
    values, rows, cols = triangle_parts(first, shape)
    diagonal = jnp.exp(jax.random.uniform(second, shape, jnp.float32, math.log(0.5), math.log(2.0)))
    below = jnp.where(cols < rows, values, 0.0)
    return (below + jnp.where(cols == rows, diagonal, 0.0)).astype(jnp.bfloat16)


def touch_ends(array, stream_key, low, largest):
    longest = array.shape.index(max(array.shape))
    spots = []
    for shift in (0, 1):
        where = [jax.random.randint(jax.random.fold_in(stream_key, axis), (), 0, length) for axis, length in enumerate(array.shape)]
        where[longest] = (where[longest] + shift) % array.shape[longest]
        spots.append(tuple(where))
    return array.at[spots[0]].set(low).at[spots[1]].set(largest)


def level_of(key, shape, cuts, low, largest):
    def one(dim, parts):
        draws = jax.random.uniform(jax.random.fold_in(jax.random.fold_in(key, 6), dim), (parts,), jnp.float32, low / len(cuts), largest / len(cuts))
        return jnp.repeat(jnp.exp(draws), shape[dim] // parts).reshape((-1,) + (1,) * (len(shape) - dim - 1))

    factor_of = one(*cuts[0])
    for cut in cuts[1:]:
        factor_of = factor_of * one(*cut)
    return factor_of


def cumulative_ranks(amount, skew):
    loads = [(1 << 20) // math.isqrt(standing ** skew) + 1 for standing in range(1, amount + 1)]
    width = 1 + sum(loads) // (1 << 30)
    return np.cumsum(np.array([max(1, weight // width) for weight in loads]))


def ranked(key, dims, number_of, lean):
    table = cumulative_ranks(number_of, lean)
    ticket = jax.random.randint(jax.random.fold_in(key, 1), dims, 0, int(table[number_of - 1]))
    rank = jnp.searchsorted(jnp.asarray(table, jnp.int32), ticket, side="right")
    return jax.random.permutation(jax.random.fold_in(key, 2), number_of)[rank].astype(jnp.int32)


def scatter_about(rng, shape, width, limit, cuts=(), kind=jnp.bfloat16):
    array = jax.random.normal(rng, shape, jnp.float32) * width
    if len(cuts) > 0:
        array = level_of(rng, shape, cuts, -0.22, 0.18) * array
    return jnp.clip(array, min=-limit, max=limit).astype(kind)


def setup_inputs(seed: int = 0) -> dict:
    arg_keys = jax.random.split(jax.random.key(seed), 11)
    return {
        "right_side": scatter_about(arg_keys[0], (LEVELS, N_PROW, N_PCOL, R, W), 1.0, 6.0, ((1, 16), (2, 32)), jnp.float32),
        "live_width": touch_ends(jax.random.randint(arg_keys[1], (LEVELS, N_PROW, N_PCOL), W // 4, W + 1), jax.random.fold_in(arg_keys[1], 1), W // 4, W).astype(jnp.int32),
        "lower_inverse": draw_lower_inverse(jax.random.fold_in(arg_keys[10], 71), 0),
        "upper_inverse": draw_upper_inverse(jax.random.fold_in(arg_keys[10], 71), 0),
        "lower_blocks": scatter_about(arg_keys[4], (PAIRS, N_PROW, N_PCOL, CAP, W, W), (0.3 / W ** 0.5), 0.109375, ((1, 16), (2, 32))),
        "lower_source": touch_ends(jax.random.randint(arg_keys[5], (PAIRS, N_PROW, N_PCOL, CAP), 0, N_PCOL), jax.random.fold_in(arg_keys[5], 1), 0, N_PCOL - 1).astype(jnp.int32),
        "lower_target": touch_ends(ranked(arg_keys[6], (PAIRS, N_PROW, N_PCOL, CAP), N_PROW, 2), jax.random.fold_in(arg_keys[6], 3), 0, N_PROW - 1).astype(jnp.int32),
        "upper_blocks": scatter_about(arg_keys[7], (PAIRS, N_PROW, N_PCOL, CAP, W, W), (0.3 / W ** 0.5), 0.109375, ((1, 16), (2, 32))),
        "upper_source": touch_ends(jax.random.randint(arg_keys[8], (PAIRS, N_PROW, N_PCOL, CAP), 0, N_PCOL), jax.random.fold_in(arg_keys[8], 1), 0, N_PCOL - 1).astype(jnp.int32),
        "upper_target": touch_ends(ranked(arg_keys[9], (PAIRS, N_PROW, N_PCOL, CAP), N_PROW, 2), jax.random.fold_in(arg_keys[9], 3), 0, N_PROW - 1).astype(jnp.int32),
    }


def pair_list(levels):
    return [(low, high) for low in range(levels) for high in range(low + 1, levels)]


def spread(rounded, blocks, source, target):
    def one_row(carry, inputs):
        row_values, row_blocks, row_source, row_target = inputs
        picked = jnp.take(row_values, row_source, axis=0)
        product = jnp.einsum("ckrw,ckwv->ckrv", picked.astype(jnp.float32), row_blocks.astype(jnp.float32), precision=lax.Precision.HIGHEST)
        placing = (row_target[:, :, None] == jnp.arange(N_PROW, dtype=jnp.int32)).astype(jnp.float32)
        term = jnp.einsum("ckq,ckrv->qcrv", placing, product, precision=lax.Precision.HIGHEST)
        return carry + term, None
    start = jnp.zeros(rounded.shape, jnp.float32)
    total, unused = lax.scan(one_row, start, (rounded, blocks, source, target))
    return total


def solve_level(residual, inverse, mask):
    product = jnp.einsum("abrw,abwv->abrv", residual.astype(jnp.bfloat16).astype(jnp.float32), inverse.astype(jnp.float32), precision=lax.Precision.HIGHEST)
    return mask * product


def reference(right_side, live_width, lower_inverse, upper_inverse, lower_blocks, lower_source, lower_target, upper_blocks, upper_source, upper_target):
    pairs = pair_list(LEVELS)
    columns = jnp.arange(W, dtype=jnp.int32)
    live_mask = (columns < live_width[..., None]).astype(jnp.float32)[:, :, :, None, :]
    sums = [jnp.zeros(right_side.shape[1:], jnp.float32) for level in range(LEVELS)]
    forward = []
    for level in range(LEVELS):
        solved = solve_level(right_side[level] - sums[level], lower_inverse[level], live_mask[level])
        forward.append(solved)
        rounded = solved.astype(jnp.bfloat16)
        for index, pair in enumerate(pairs):
            if pair[0] == level:
                sums[pair[1]] = sums[pair[1]] + spread(rounded, lower_blocks[index], lower_source[index], lower_target[index])
    sums = [jnp.zeros(right_side.shape[1:], jnp.float32) for level in range(LEVELS)]
    backward = [None] * LEVELS
    for level in reversed(range(LEVELS)):
        solved = solve_level(forward[level] - sums[level], upper_inverse[level], live_mask[level])
        backward[level] = solved
        rounded = solved.astype(jnp.bfloat16)
        for index, pair in enumerate(pairs):
            if pair[1] == level:
                sums[pair[0]] = sums[pair[0]] + spread(rounded, upper_blocks[index], upper_source[index], upper_target[index])
    return jnp.stack(forward), jnp.stack(backward)
```

```python
import functools

import jax
import jax.numpy as jnp
from jax import lax
from jax.experimental import pallas as pl
from jax.experimental.pallas import tpu as pltpu
from jax.sharding import PartitionSpec as P


MESH = pl.DeviceIdType.MESH
NX = 4
CORES = 2
ROWS = 16
LANES = 128
SLOTS = 4
BF16 = jnp.bfloat16
F32 = jnp.float32
LOW_SOURCE, LOW_TARGET, UP_SOURCE, UP_TARGET, LIVE = 0, 12, 24, 36, 48


def kernel(
    ny,
    nz,
    rhs,
    live_width,
    low_source,
    low_target,
    up_source,
    up_target,
    inv_low,
    inv_up,
    blk_low,
    blk_up,
    out_f,
    out_b,
    rhs_first,
    rhs_rest,
    w_inv_low,
    w_inv_up,
    w_low,
    w_up,
    x_first,
    xf,
    yb,
    piece,
    held,
    stage,
    pick,
    prod,
    acc,
    part,
    landed,
    tabs,
    stab,
    local_sem,
    pair_send,
    pair_recv,
    tab_send,
    tab_recv,
    tab_local,
    spread_send,
    spread_recv,
    pick_send,
    pick_recv,
    sum_send,
    sum_recv,
    out_local,
    out_send,
    out_recv,
):
    prow, pcol = lax.axis_index("prow"), lax.axis_index("pcol")
    z, c = prow // CORES, prow % CORES
    y, x = pcol // NX, pcol % NX
    other = 1 - c
    n_plane = ny * NX

    def at(zz, cc, yy, xx):
        return {"prow": zz * CORES + cc, "pcol": yy * NX + xx}

    def remote(src, dst, send, recv, where):
        return pltpu.make_async_remote_copy(
            src_ref=src, dst_ref=dst, send_sem=send, recv_sem=recv, device_id=where, device_id_type=MESH
        )

    partner = at(z, other, y, x)
    mine = pl.ds(pl.multiple_of(c * 2 * ROWS, 2 * ROWS), 2 * ROWS)
    theirs = pl.ds(pl.multiple_of(other * 2 * ROWS, 2 * ROWS), 2 * ROWS)

    first_rhs = pltpu.make_async_copy(rhs.at[0], rhs_first, local_sem.at[0])
    first_inv = pltpu.make_async_copy(inv_low.at[0], w_inv_low.at[0, 0], local_sem.at[1])
    first_rhs.start()
    first_inv.start()
    own = []
    shared = []

    def both(src, dst_own, dst_partner, src_partner=None):
        n = len(own)
        own.append(pltpu.make_async_copy(src, dst_own, local_sem.at[2 + n]))
        own[-1].start()
        shared.append(
            remote(src if src_partner is None else src_partner, dst_partner, pair_send.at[1 + n], pair_recv.at[1 + n], partner)
        )
        return n

    got = {}
    got["low", 0] = both(blk_low.at[0], w_low.at[0, 0], w_low.at[0, 1])
    got["low", 1] = both(blk_low.at[1], w_low.at[1, 0], w_low.at[1, 1])
    got["rhs"] = both(rhs.at[pl.ds(1, 2), mine], rhs_rest.at[0], rhs_rest.at[1], rhs.at[pl.ds(1, 2), theirs])
    got["inv_low"] = both(inv_low.at[pl.ds(1, 2)], w_inv_low.at[pl.ds(1, 2), 0], w_inv_low.at[pl.ds(1, 2), 1])
    got["low", 2] = both(blk_low.at[2], w_low.at[2, 0], w_low.at[2, 1])
    got["inv_up"] = both(inv_up, w_inv_up.at[:, 0], w_inv_up.at[:, 1])
    got["up", 2] = both(blk_up.at[2], w_up.at[2, 0], w_up.at[2, 1])
    got["up", 1] = both(blk_up.at[1], w_up.at[1, 0], w_up.at[1, 1])
    got["up", 0] = both(blk_up.at[0], w_up.at[0, 0], w_up.at[0, 1])

    spot = lax.broadcasted_iota(jnp.int32, (8, LANES), 1)
    row = jnp.zeros((8, LANES), jnp.int32)
    for base, small in ((LOW_SOURCE, low_source), (LOW_TARGET, low_target), (UP_SOURCE, up_source), (UP_TARGET, up_target)):
        for pair in range(3):
            for k in range(SLOTS):
                row = jnp.where(spot == base + SLOTS * pair + k, small[pair, 0, 0, k], row)
    for level in range(3):
        row = jnp.where(spot == LIVE + level, live_width[level], row)
    tabs[0, x] = row

    def need(name):
        own[got[name]].wait()
        shared[got[name]].wait_recv()

    barrier = pltpu.get_barrier_semaphore()

    def hello(where):
        pl.semaphore_signal(barrier, inc=1, device_id=where, device_id_type=MESH)

    def far(index, count):
        step = (index + 1) // 2
        return count // 2 + step * (1 - 2 * (index % 2))

    def plane_loop(act):
        def row(i, carry):
            yy = lax.rem(y + far(i, ny), ny)
            for dx in (2, 1, 3, 0):
                act(yy, lax.rem(x + dx, NX))
            return carry

        lax.fori_loop(0, ny - 1, row, 0)
        for dx in (2, 1, 3):
            act(y, lax.rem(x + dx, NX))

    plane_loop(lambda yy, xx: hello(at(z, c, yy, xx)))

    def hello_z(i, carry):
        hello(at(lax.rem(z + far(i, nz), nz), c, y, x))
        return carry

    lax.fori_loop(0, nz - 1, hello_z, 0)
    for dx in range(NX):
        hello(at(z, other, y, lax.rem(x + dx, NX)))

    lane = lax.broadcasted_iota(jnp.int32, (1, 2 * LANES), 1)

    def live_mask(width):
        return (lane < width).astype(F32)

    def dot(left, right):
        return jnp.dot(left, right, preferred_element_type=F32)

    first_rhs.wait()
    first_inv.wait()
    x_first[...] = live_mask(live_width[0]) * dot(rhs_first[...].astype(BF16), w_inv_low[0, 0])
    xf[0, 0] = x_first[mine, :]
    first_out = pltpu.make_async_copy(x_first, out_f.at[0], out_local.at[0])
    first_out.start()

    pl.semaphore_wait(barrier, (n_plane - 1) + (nz - 1) + NX)
    first_x = remote(x_first.at[theirs], xf.at[0, 1], pair_send.at[0], pair_recv.at[0], partner)
    first_x.start()

    tab_copies = []
    for a in range(CORES):
        for dx in range(NX):
            if (a, dx) != (0, 0):
                tab_copies.append(
                    remote(
                        tabs.at[0, x],
                        tabs.at[a, x],
                        tab_send.at[len(tab_copies)],
                        tab_recv.at[len(tab_copies)],
                        at(z, c if a == 0 else other, y, lax.rem(x + dx, NX)),
                    )
                )
                tab_copies[-1].start()
    for copy in shared[:2]:
        copy.start()

    me = y * NX + x

    def spread(t, r, values):
        for a in range(CORES):
            rounded = values[a].astype(BF16)
            for h in range(2):
                piece[t, r, 2 * a + h] = rounded[:, h * LANES : (h + 1) * LANES]

        def send(yy, xx):
            remote(
                piece.at[t, r, xx], held[2 * t + r].at[me], spread_send.at[t, r], spread_recv.at[t, r], at(z, c, yy, xx)
            ).start()

        plane_loop(send)
        held[2 * t + r][me] = piece[t, r, x]

    def spread_done(t, r):
        span = held[2 * t + r].at[pl.ds(0, n_plane - 1)]
        remote(span, span, spread_send.at[t, r], spread_recv.at[t, r], partner).wait_recv()

    def choose(t, r, n, base):
        a = x // 2
        for d in (2, 1, 3, 0):
            xx = lax.rem(x + d, NX)
            for k in range(SLOTS):
                tile = held[2 * t + r][stab[a, xx, 0, base + k]]
                if d:
                    stage[t, r, n, d - 1, k] = tile
                else:
                    pick[t, r, n, x, k] = tile
            if d:
                remote(
                    stage.at[t, r, n, d - 1], pick.at[t, r, n, x], pick_send.at[t, r, n], pick_recv.at[t, r, n], at(z, c, y, xx)
                ).start()

    def choose_done(t, r, n):
        span = pick.at[t, r, n, pl.ds(0, NX - 1)]
        remote(span, span, pick_send.at[t, r, n], pick_recv.at[t, r, n], partner).wait_recv()

    def products(t, r, n, weights, pair):
        for a in range(CORES):
            for k in range(SLOTS):
                left = jnp.concatenate([pick[t, r, n, 2 * a, k], pick[t, r, n, 2 * a + 1, k]], axis=1)
                prod[a * SLOTS + k] = dot(left, weights[pair, a, k])

    def placed(base, q):
        total = None
        for a in range(CORES):
            for k in range(SLOTS):
                hit = jnp.where(stab[a, x, 0, base + k] == q, 1.0, 0.0).astype(F32)
                term = prod[a * SLOTS + k] * hit
                total = term if total is None else total + term
        return total

    def target_of(d, a):
        return CORES * lax.rem(z + d, nz) + (c if a == 0 else other)

    def keep(r, base):
        def one(d, carry):
            for a in range(CORES):
                acc[r, d, a] = placed(base, target_of(d, a))
            return carry

        lax.fori_loop(0, nz, one, 0)

    def exchange(t, r, base, with_kept):
        def value(d, a):
            total = placed(base, target_of(d, a))
            return total + acc[r, d, a] if with_kept else total

        def one(i, carry):
            d = far(i, nz)
            for a in range(CORES):
                part[t, r, d - 1, a] = value(d, a).astype(BF16)
            remote(
                part.at[t, r, d - 1],
                landed.at[t, r, d - 1],
                sum_send.at[t, r],
                sum_recv.at[t, r],
                at(lax.rem(z + d, nz), c, y, x),
            ).start()
            return carry

        lax.fori_loop(0, nz - 1, one, 0)
        return [value(0, a) for a in range(CORES)]

    def summed(t, r, kept):
        remote(landed.at[t, r], landed.at[t, r], sum_send.at[t, r], sum_recv.at[t, r], partner).wait_recv()
        totals = []
        for a in range(CORES):
            total = kept[a]
            for d in range(nz - 1):
                total = total + landed[t, r, d, a].astype(F32)
            totals.append(total)
        return totals

    masks = {}

    def mask(level, a):
        if (level, a) not in masks:
            masks[level, a] = live_mask(stab[a, x, 0, LIVE + level])
        return masks[level, a]

    def solve(level, weights, residual):
        return [mask(level, a) * dot(residual[a].astype(BF16), weights[level, a]) for a in range(CORES)]

    def rows(r):
        return slice(r * ROWS, (r + 1) * ROWS)

    out_copies = []

    def put(out, values, level):
        n = len(out_copies) // 2
        out_copies.append(pltpu.make_async_copy(values.at[level, 0], out.at[level, mine], out_local.at[1 + n]))
        out_copies.append(remote(values.at[level, 1], out.at[level, mine], out_send.at[n], out_recv.at[n], partner))
        out_copies[-2].start()
        out_copies[-1].start()

    chunks = range(2)

    first_x.wait_recv()
    for r in chunks:
        spread(0, r, [xf[0, a, rows(r)] for a in range(CORES)])
    for copy in shared[2:]:
        copy.start()
    for copy in tab_copies:
        copy.wait_recv()
    to_scalar = pltpu.make_async_copy(tabs, stab, tab_local)
    to_scalar.start()
    to_scalar.wait()

    def round_of(t, weights, name, base_source, base_target, crit, late, with_kept):
        for r in chunks:
            spread_done(t, r)
            choose(t, r, 0, base_source + SLOTS * crit)
        if late is not None:
            for r in chunks:
                choose(t, r, 1, base_source + SLOTS * late)
        kept = []
        need((name, crit))
        for r in chunks:
            choose_done(t, r, 0)
            products(t, r, 0, weights, crit)
            kept.append(exchange(t, r, base_target + SLOTS * crit, with_kept))
        if late is not None:
            need((name, late))
            for r in chunks:
                choose_done(t, r, 1)
                products(t, r, 1, weights, late)
                keep(r, base_target + SLOTS * late)
        return kept

    kept = round_of(0, w_low, "low", LOW_SOURCE, LOW_TARGET, 0, 1, False)
    need("rhs")
    need("inv_low")
    for r in chunks:
        total = summed(0, r, kept[r])
        solved = solve(1, w_inv_low, [rhs_rest[a, 0, rows(r)] - total[a] for a in range(CORES)])
        spread(1, r, solved)
        for a in range(CORES):
            xf[1, a, rows(r)] = solved[a]
    put(out_f, xf, 1)

    kept = round_of(1, w_low, "low", LOW_SOURCE, LOW_TARGET, 2, None, True)
    need("inv_up")
    for r in chunks:
        total = summed(1, r, kept[r])
        solved = solve(2, w_inv_low, [rhs_rest[a, 1, rows(r)] - total[a] for a in range(CORES)])
        back = solve(2, w_inv_up, solved)
        spread(2, r, back)
        for a in range(CORES):
            xf[2, a, rows(r)] = solved[a]
            yb[2, a, rows(r)] = back[a]
    put(out_f, xf, 2)
    put(out_b, yb, 2)

    kept = round_of(2, w_up, "up", UP_SOURCE, UP_TARGET, 2, 1, False)
    for r in chunks:
        total = summed(2, r, kept[r])
        back = solve(1, w_inv_up, [xf[1, a, rows(r)] - total[a] for a in range(CORES)])
        spread(3, r, back)
        for a in range(CORES):
            yb[1, a, rows(r)] = back[a]
    put(out_b, yb, 1)

    kept = round_of(3, w_up, "up", UP_SOURCE, UP_TARGET, 0, None, True)
    for r in chunks:
        total = summed(3, r, kept[r])
        back = solve(0, w_inv_up, [xf[0, a, rows(r)] - total[a] for a in range(CORES)])
        for a in range(CORES):
            yb[0, a, rows(r)] = back[a]
    put(out_b, yb, 0)

    first_out.wait()
    first_x.wait_send()
    for copy in shared + tab_copies:
        copy.wait_send()
    for t in range(4):
        for r in chunks:
            span = held[2 * t + r].at[pl.ds(0, n_plane - 1)]
            remote(span, span, spread_send.at[t, r], spread_recv.at[t, r], partner).wait_send()
            for n in range(2 if t % 2 == 0 else 1):
                span = pick.at[t, r, n, pl.ds(0, NX - 1)]
                remote(span, span, pick_send.at[t, r, n], pick_recv.at[t, r, n], partner).wait_send()
            remote(landed.at[t, r], landed.at[t, r], sum_send.at[t, r], sum_recv.at[t, r], partner).wait_send()
    for copy in out_copies:
        copy.wait()


def deliver(forward, backward, out_f, out_b, sem):
    copies = [
        pltpu.make_async_copy(src.at[level], dst.at[level], sem.at[n, level])
        for n, (src, dst) in enumerate(((forward, out_f), (backward, out_b)))
        for level in range(3)
    ]
    for copy in copies:
        copy.start()
    for copy in copies:
        copy.wait()


def local(
    ny,
    nz,
    right_side,
    live_width,
    lower_inverse,
    upper_inverse,
    lower_blocks,
    lower_source,
    lower_target,
    upper_blocks,
    upper_source,
    upper_target,
):
    levels, _, _, count, width = right_side.shape
    n_plane = ny * NX
    dma = pltpu.SemaphoreType.DMA
    hbm = pl.BlockSpec(memory_space=pl.ANY)
    out = jax.ShapeDtypeStruct((levels, count, width), F32)
    forward, backward = pl.pallas_call(
        functools.partial(kernel, ny, nz),
        out_shape=(pltpu.VMEM(out.shape, F32), pltpu.VMEM(out.shape, F32)),
        in_specs=[hbm] + [pl.BlockSpec(memory_space=pltpu.SMEM)] * 5 + [hbm] * 4,
        out_specs=(hbm, hbm),
        scratch_shapes=[
            pltpu.VMEM((count, width), F32),
            pltpu.VMEM((CORES, levels - 1, 2 * ROWS, width), F32),
            pltpu.VMEM((levels, CORES, width, width), BF16),
            pltpu.VMEM((levels, CORES, width, width), BF16),
            pltpu.VMEM((levels, CORES, SLOTS, width, width), BF16),
            pltpu.VMEM((levels, CORES, SLOTS, width, width), BF16),
            pltpu.VMEM((count, width), F32),
            pltpu.VMEM((levels, CORES, 2 * ROWS, width), F32),
            pltpu.VMEM((levels, CORES, 2 * ROWS, width), F32),
            pltpu.VMEM((4, 2, NX, ROWS, LANES), BF16),
            [pltpu.VMEM((n_plane, ROWS, LANES), BF16) for _ in range(8)],
            pltpu.VMEM((4, 2, 2, NX - 1, SLOTS, ROWS, LANES), BF16),
            pltpu.VMEM((4, 2, 2, NX, SLOTS, ROWS, LANES), BF16),
            pltpu.VMEM((CORES * SLOTS, ROWS, width), F32),
            pltpu.VMEM((2, nz, CORES, ROWS, width), F32),
            pltpu.VMEM((4, 2, nz - 1, CORES, ROWS, width), BF16),
            pltpu.VMEM((4, 2, nz - 1, CORES, ROWS, width), BF16),
            pltpu.VMEM((CORES, NX, 8, LANES), jnp.int32),
            pltpu.SMEM((CORES, NX, 8, LANES), jnp.int32),
            dma((11,)),
            dma((10,)),
            dma((10,)),
            dma((7,)),
            dma((7,)),
            dma(()),
            dma((4, 2)),
            dma((4, 2)),
            dma((4, 2, 2)),
            dma((4, 2, 2)),
            dma((4, 2)),
            dma((4, 2)),
            dma((6,)),
            dma((5,)),
            dma((5,)),
        ],
        compiler_params=pltpu.CompilerParams(collective_id=0, has_side_effects=True, vmem_limit_bytes=60 << 20),
        cost_estimate=pl.CostEstimate(flops=252 << 20, bytes_accessed=8 << 20, transcendentals=0),
    )(
        right_side.reshape(levels, count, width),
        live_width.reshape(levels),
        lower_source,
        lower_target,
        upper_source,
        upper_target,
        lower_inverse.reshape(levels, width, width),
        upper_inverse.reshape(levels, width, width),
        lower_blocks.reshape(levels, SLOTS, width, width),
        upper_blocks.reshape(levels, SLOTS, width, width),
    )
    forward, backward = pl.pallas_call(
        deliver,
        out_shape=(out, out),
        in_specs=[pl.BlockSpec(memory_space=pltpu.VMEM), pl.BlockSpec(memory_space=pltpu.VMEM)],
        out_specs=(hbm, hbm),
        scratch_shapes=[dma((2, 3))],
        compiler_params=pltpu.CompilerParams(vmem_limit_bytes=1 << 20),
        cost_estimate=pl.CostEstimate(flops=0, bytes_accessed=1 << 20, transcendentals=0),
    )(forward, backward)
    return forward[:, None, None], backward[:, None, None]


def solution(mesh):
    placed = (
        P(None, "prow", "pcol", None, None),
        P(None, "prow", "pcol"),
        P(None, "prow", "pcol", None, None),
        P(None, "prow", "pcol", None, None),
        P(None, "prow", "pcol", None, None, None),
        P(None, "prow", "pcol", None),
        P(None, "prow", "pcol", None),
        P(None, "prow", "pcol", None, None, None),
        P(None, "prow", "pcol", None),
        P(None, "prow", "pcol", None),
    )
    return jax.shard_map(
        functools.partial(local, mesh.shape["pcol"] // NX, mesh.shape["prow"] // CORES),
        mesh=mesh,
        in_specs=placed,
        out_specs=(P(None, "prow", "pcol", None, None), P(None, "prow", "pcol", None, None)),
        check_vma=False,
    )
```

```python
import functools

import jax
import jax.numpy as jnp
from jax import lax
from jax.experimental import pallas as pl
from jax.experimental.pallas import tpu as pltpu
from jax.sharding import PartitionSpec as P


MESH = pl.DeviceIdType.MESH
NX = 4
CORES = 2
CHUNKS = 4
PART = 8
ROWS = CORES * PART
LANES = 128
SLOTS = 4
BF16 = jnp.bfloat16
F32 = jnp.float32
LOW_SOURCE, LOW_TARGET, UP_SOURCE, UP_TARGET, LIVE = 0, 12, 24, 36, 48


def kernel(
    ny,
    nz,
    rhs,
    live_width,
    low_source,
    low_target,
    up_source,
    up_target,
    inv_low,
    inv_up,
    blk_low,
    blk_up,
    out_f,
    out_b,
    rhs_first,
    rhs_rest,
    w_inv_low,
    w_inv_up,
    w_low,
    w_up,
    x_first,
    xf,
    yb,
    piece,
    held,
    stage,
    pick,
    prod,
    acc,
    mine_sum,
    part,
    landed,
    tabs,
    stab,
    local_sem,
    pair_send,
    pair_recv,
    tab_send,
    tab_recv,
    tab_local,
    spread_send,
    spread_recv,
    pick_send,
    pick_recv,
    sum_send,
    sum_recv,
    out_local,
    out_send,
    out_recv,
):
    prow, pcol = lax.axis_index("prow"), lax.axis_index("pcol")
    z, c = prow // CORES, prow % CORES
    y, x = pcol // NX, pcol % NX
    other = 1 - c

    def at(zz, cc, yy, xx):
        return {"prow": zz * CORES + cc, "pcol": yy * NX + xx}

    def remote(src, dst, send, recv, where):
        return pltpu.make_async_remote_copy(
            src_ref=src, dst_ref=dst, send_sem=send, recv_sem=recv, device_id=where, device_id_type=MESH
        )

    partner = at(z, other, y, x)
    mine = pl.ds(pl.multiple_of(c * CHUNKS * PART, CHUNKS * PART), CHUNKS * PART)
    theirs = pl.ds(pl.multiple_of(other * CHUNKS * PART, CHUNKS * PART), CHUNKS * PART)

    barrier = pltpu.get_barrier_semaphore()

    def hello(where):
        pl.semaphore_signal(barrier, inc=1, device_id=where, device_id_type=MESH)

    def far(index, count):
        step = (index + 1) // 2
        return count // 2 + step * (1 - 2 * (index % 2))

    def ring(act, count):
        def one(i, carry):
            act(far(i, count))
            return carry

        lax.fori_loop(0, count - 1, one, 0)

    ring(lambda d: hello(at(z, c, lax.rem(y + d, ny), x)), ny)
    ring(lambda d: hello(at(lax.rem(z + d, nz), c, y, x)), nz)
    for dx in range(1, NX):
        hello(at(z, c, y, lax.rem(x + dx, NX)))
    for dx in range(NX):
        hello(at(z, other, y, lax.rem(x + dx, NX)))

    first_rhs = pltpu.make_async_copy(rhs.at[0], rhs_first, local_sem.at[0])
    first_inv = pltpu.make_async_copy(inv_low.at[0], w_inv_low.at[0, 0], local_sem.at[1])
    first_rhs.start()
    first_inv.start()
    own = []
    shared = []

    def both(src, dst_own, dst_partner, src_partner=None):
        n = len(own)
        own.append(pltpu.make_async_copy(src, dst_own, local_sem.at[2 + n]))
        own[-1].start()
        shared.append(
            remote(src if src_partner is None else src_partner, dst_partner, pair_send.at[1 + n], pair_recv.at[1 + n], partner)
        )
        return n

    got = {}
    got["low", 0] = both(blk_low.at[0], w_low.at[0, 0], w_low.at[0, 1])
    got["low", 1] = both(blk_low.at[1], w_low.at[1, 0], w_low.at[1, 1])
    got["rhs"] = both(rhs.at[pl.ds(1, 2), mine], rhs_rest.at[0], rhs_rest.at[1], rhs.at[pl.ds(1, 2), theirs])
    got["inv_low"] = both(inv_low.at[pl.ds(1, 2)], w_inv_low.at[pl.ds(1, 2), 0], w_inv_low.at[pl.ds(1, 2), 1])
    got["low", 2] = both(blk_low.at[2], w_low.at[2, 0], w_low.at[2, 1])
    got["inv_up"] = both(inv_up, w_inv_up.at[:, 0], w_inv_up.at[:, 1])
    got["up", 2] = both(blk_up.at[2], w_up.at[2, 0], w_up.at[2, 1])
    got["up", 1] = both(blk_up.at[1], w_up.at[1, 0], w_up.at[1, 1])
    got["up", 0] = both(blk_up.at[0], w_up.at[0, 0], w_up.at[0, 1])

    spot = lax.broadcasted_iota(jnp.int32, (8, LANES), 1)
    row = jnp.zeros((8, LANES), jnp.int32)
    for base, small in ((LOW_SOURCE, low_source), (LOW_TARGET, low_target), (UP_SOURCE, up_source), (UP_TARGET, up_target)):
        for pair in range(3):
            for k in range(SLOTS):
                row = jnp.where(spot == base + SLOTS * pair + k, small[pair, 0, 0, k], row)
    for level in range(3):
        row = jnp.where(spot == LIVE + level, live_width[level], row)
    tabs[0, x] = row

    def need(name):
        own[got[name]].wait()
        shared[got[name]].wait_recv()

    lane = lax.broadcasted_iota(jnp.int32, (1, 2 * LANES), 1)

    def live_mask(width):
        return (lane < width).astype(F32)

    def dot(left, right):
        return jnp.dot(left, right, preferred_element_type=F32)

    first_rhs.wait()
    first_inv.wait()
    x_first[...] = live_mask(live_width[0]) * dot(rhs_first[...].astype(BF16), w_inv_low[0, 0])
    xf[0, 0] = x_first[mine, :]
    first_out = pltpu.make_async_copy(x_first, out_f.at[0], out_local.at[0])
    first_out.start()

    pl.semaphore_wait(barrier, (ny - 1) + (nz - 1) + (NX - 1) + NX)
    first_x = remote(x_first.at[theirs], xf.at[0, 1], pair_send.at[0], pair_recv.at[0], partner)
    first_x.start()

    tab_copies = []
    for a in range(CORES):
        for dx in range(NX):
            if (a, dx) != (0, 0):
                tab_copies.append(
                    remote(
                        tabs.at[0, x],
                        tabs.at[a, x],
                        tab_send.at[len(tab_copies)],
                        tab_recv.at[len(tab_copies)],
                        at(z, c if a == 0 else other, y, lax.rem(x + dx, NX)),
                    )
                )
                tab_copies[-1].start()
    for copy in shared[:2]:
        copy.start()

    def halves(own_rows, partner_rows):
        return jnp.concatenate([own_rows, partner_rows], axis=0)

    def rows(r):
        return slice(r * PART, (r + 1) * PART)

    def chunk(ref, r, *place):
        return halves(ref[(0, *place, rows(r))], ref[(1, *place, rows(r))])

    def spread(t, r, tile):
        piece[t, r] = tile.astype(BF16)
        ring(
            lambda d: remote(
                piece.at[t, r],
                held[CHUNKS * t + r].at[y],
                spread_send.at[t, r],
                spread_recv.at[t, r],
                at(z, c, lax.rem(y + d, ny), x),
            ).start(),
            ny,
        )
        held[CHUNKS * t + r][y] = tile.astype(BF16)

    def spread_all(t, r):
        span = held[CHUNKS * t + r].at[pl.ds(0, ny - 1)]
        return remote(span, span, spread_send.at[t, r], spread_recv.at[t, r], partner)

    def choose(t, r, n, base):
        have = held[CHUNKS * t + r]
        for d in (2, 1, 3, 0):
            xx = lax.rem(x + d, NX)
            for k in range(SLOTS):
                top, low = [have[lax.div(stab[a, xx, 0, base + k], NX)].astype(F32) for a in range(CORES)]
                tile = halves(top[:PART], low[PART:]).astype(BF16)
                if d:
                    stage[t, r, n, d - 1, k] = tile
                else:
                    pick[(CHUNKS * t + r) * 2 + n][x, k] = tile
            if d:
                remote(
                    stage.at[t, r, n, d - 1],
                    pick[(CHUNKS * t + r) * 2 + n].at[x],
                    pick_send.at[t, r, n],
                    pick_recv.at[t, r, n],
                    at(z, c, y, xx),
                ).start()

    def choose_all(t, r, n):
        span = pick[(CHUNKS * t + r) * 2 + n].at[pl.ds(0, NX - 1)]
        return remote(span, span, pick_send.at[t, r, n], pick_recv.at[t, r, n], partner)

    def products(t, r, n, weights, pair, base):
        choose_all(t, r, n).wait_recv()
        for a in range(CORES):
            for k in range(SLOTS):
                column = lax.rem(stab[a, x, 0, base + k], NX)
                left = pick[(CHUNKS * t + r) * 2 + n][column, k]
                prod[a * SLOTS + k] = dot(left, weights[pair, a, k])[a * PART : (a + 1) * PART]

    def placed(base, d):
        zz = CORES * lax.rem(z + d, nz)
        totals = []
        for to, q in enumerate((zz + c, zz + other)):
            total = None
            for a in range(CORES):
                for k in range(SLOTS):
                    hit = jnp.where(stab[a, x, 0, base + k] == q, 1.0, 0.0).astype(F32)
                    term = prod[a * SLOTS + k] * hit
                    total = term if total is None else total + term
            totals.append(total)
        return halves(*totals)

    def keep(r, base):
        def one(d, carry):
            acc[r, d] = placed(base, d)
            return carry

        lax.fori_loop(0, nz, one, 0)

    def exchange(t, r, base, with_kept):
        def value(d):
            return placed(base, d) + acc[r, d] if with_kept else placed(base, d)

        def send(d):
            part[t, r, d - 1] = value(d).astype(BF16)
            remote(
                part.at[t, r, d - 1],
                landed.at[t, r, d - 1],
                sum_send.at[t, r],
                sum_recv.at[t, r],
                at(lax.rem(z + d, nz), c, y, x),
            ).start()

        ring(send, nz)
        mine_sum[r] = value(0)

    def sum_all(t, r):
        return remote(landed.at[t, r], landed.at[t, r], sum_send.at[t, r], sum_recv.at[t, r], partner)

    def summed(t, r):
        sum_all(t, r).wait_recv()
        total = mine_sum[r]
        for d in range(nz - 1):
            total = total + landed[t, r, d].astype(F32)
        return total

    in_own = lax.broadcasted_iota(jnp.int32, (ROWS, 2 * LANES), 0) < PART
    in_lane = lax.broadcasted_iota(jnp.int32, (ROWS, 2 * LANES), 1)

    def solve(level, weights, residual):
        residual = residual.astype(BF16)
        top, low = [dot(residual, weights[level, a]) for a in range(CORES)]
        width = jnp.where(in_own, stab[0, x, 0, LIVE + level], stab[1, x, 0, LIVE + level])
        return (in_lane < width).astype(F32) * halves(top[:PART], low[PART:])

    def store(ref, level, r, tile):
        for a in range(CORES):
            ref[level, a, rows(r)] = tile[a * PART : (a + 1) * PART]

    out_copies = []

    def put(out, values, level):
        n = len(out_copies) // 2
        out_copies.append(pltpu.make_async_copy(values.at[level, 0], out.at[level, mine], out_local.at[1 + n]))
        out_copies.append(remote(values.at[level, 1], out.at[level, mine], out_send.at[n], out_recv.at[n], partner))
        out_copies[-2].start()
        out_copies[-1].start()

    chunks = range(CHUNKS)

    first_x.wait_recv()
    for r in chunks:
        spread(0, r, chunk(xf.at[0], r))
    for copy in shared[2:]:
        copy.start()
    for copy in tab_copies:
        copy.wait_recv()
    to_scalar = pltpu.make_async_copy(tabs, stab, tab_local)
    to_scalar.start()
    to_scalar.wait()

    def gather(t, base, crit):
        for r in chunks:
            spread_all(t, r).wait_recv()
            choose(t, r, 0, base + SLOTS * crit)

    def multiply(t, weights, name, source, target, crit, late):
        need((name, crit))
        for r in chunks:
            products(t, r, 0, weights, crit, source + SLOTS * crit)
            exchange(t, r, target + SLOTS * crit, late is None)
            if late is not None:
                choose(t, r, 1, source + SLOTS * late)

    def multiply_late(t, r, weights, name, source, target, late):
        if r == 0:
            need((name, late))
        products(t, r, 1, weights, late, source + SLOTS * late)
        keep(r, target + SLOTS * late)

    gather(0, LOW_SOURCE, 0)
    multiply(0, w_low, "low", LOW_SOURCE, LOW_TARGET, 0, 1)
    need("rhs")
    need("inv_low")
    for r in chunks:
        solved = solve(1, w_inv_low, chunk(rhs_rest, r, 0) - summed(0, r))
        spread(1, r, solved)
        store(xf, 1, r, solved)
        multiply_late(0, r, w_low, "low", LOW_SOURCE, LOW_TARGET, 1)
    put(out_f, xf, 1)

    gather(1, LOW_SOURCE, 2)
    multiply(1, w_low, "low", LOW_SOURCE, LOW_TARGET, 2, None)
    need("inv_up")
    for r in chunks:
        solved = solve(2, w_inv_low, chunk(rhs_rest, r, 1) - summed(1, r))
        back = solve(2, w_inv_up, solved)
        spread(2, r, back)
        store(xf, 2, r, solved)
        store(yb, 2, r, back)
    put(out_f, xf, 2)
    put(out_b, yb, 2)

    gather(2, UP_SOURCE, 2)
    multiply(2, w_up, "up", UP_SOURCE, UP_TARGET, 2, 1)
    for r in chunks:
        back = solve(1, w_inv_up, chunk(xf.at[1], r) - summed(2, r))
        spread(3, r, back)
        store(yb, 1, r, back)
        multiply_late(2, r, w_up, "up", UP_SOURCE, UP_TARGET, 1)
    put(out_b, yb, 1)

    gather(3, UP_SOURCE, 0)
    multiply(3, w_up, "up", UP_SOURCE, UP_TARGET, 0, None)
    for r in chunks:
        store(yb, 0, r, solve(0, w_inv_up, chunk(xf.at[0], r) - summed(3, r)))
    put(out_b, yb, 0)

    first_out.wait()
    first_x.wait_send()
    for copy in shared + tab_copies:
        copy.wait_send()
    for t in range(4):
        for r in chunks:
            spread_all(t, r).wait_send()
            choose_all(t, r, 0).wait_send()
            if t % 2 == 0:
                choose_all(t, r, 1).wait_send()
            sum_all(t, r).wait_send()
    for copy in out_copies:
        copy.wait()


def deliver(forward, backward, out_f, out_b, sem):
    copies = [
        pltpu.make_async_copy(src.at[level], dst.at[level], sem.at[n, level])
        for n, (src, dst) in enumerate(((forward, out_f), (backward, out_b)))
        for level in range(3)
    ]
    for copy in copies:
        copy.start()
    for copy in copies:
        copy.wait()


def local(
    ny,
    nz,
    right_side,
    live_width,
    lower_inverse,
    upper_inverse,
    lower_blocks,
    lower_source,
    lower_target,
    upper_blocks,
    upper_source,
    upper_target,
):
    levels, _, _, count, width = right_side.shape
    dma = pltpu.SemaphoreType.DMA
    hbm = pl.BlockSpec(memory_space=pl.ANY)
    out = jax.ShapeDtypeStruct((levels, count, width), F32)
    forward, backward = pl.pallas_call(
        functools.partial(kernel, ny, nz),
        out_shape=(pltpu.VMEM(out.shape, F32), pltpu.VMEM(out.shape, F32)),
        in_specs=[hbm] + [pl.BlockSpec(memory_space=pltpu.SMEM)] * 5 + [hbm] * 4,
        out_specs=(hbm, hbm),
        scratch_shapes=[
            pltpu.VMEM((count, width), F32),
            pltpu.VMEM((CORES, levels - 1, CHUNKS * PART, width), F32),
            pltpu.VMEM((levels, CORES, width, width), BF16),
            pltpu.VMEM((levels, CORES, width, width), BF16),
            pltpu.VMEM((levels, CORES, SLOTS, width, width), BF16),
            pltpu.VMEM((levels, CORES, SLOTS, width, width), BF16),
            pltpu.VMEM((count, width), F32),
            pltpu.VMEM((levels, CORES, CHUNKS * PART, width), F32),
            pltpu.VMEM((levels, CORES, CHUNKS * PART, width), F32),
            pltpu.VMEM((4, CHUNKS, ROWS, width), BF16),
            [pltpu.VMEM((ny, ROWS, width), BF16) for _ in range(4 * CHUNKS)],
            pltpu.VMEM((4, CHUNKS, 2, NX - 1, SLOTS, ROWS, width), BF16),
            [pltpu.VMEM((NX, SLOTS, ROWS, width), BF16) for _ in range(8 * CHUNKS)],
            pltpu.VMEM((CORES * SLOTS, PART, width), F32),
            pltpu.VMEM((CHUNKS, nz, ROWS, width), F32),
            pltpu.VMEM((CHUNKS, ROWS, width), F32),
            pltpu.VMEM((4, CHUNKS, nz - 1, ROWS, width), BF16),
            pltpu.VMEM((4, CHUNKS, nz - 1, ROWS, width), BF16),
            pltpu.VMEM((CORES, NX, 8, LANES), jnp.int32),
            pltpu.SMEM((CORES, NX, 8, LANES), jnp.int32),
            dma((11,)),
            dma((10,)),
            dma((10,)),
            dma((7,)),
            dma((7,)),
            dma(()),
            dma((4, CHUNKS)),
            dma((4, CHUNKS)),
            dma((4, CHUNKS, 2)),
            dma((4, CHUNKS, 2)),
            dma((4, CHUNKS)),
            dma((4, CHUNKS)),
            dma((6,)),
            dma((5,)),
            dma((5,)),
        ],
        compiler_params=pltpu.CompilerParams(collective_id=0, has_side_effects=True, vmem_limit_bytes=60 << 20),
        cost_estimate=pl.CostEstimate(flops=252 << 20, bytes_accessed=8 << 20, transcendentals=0),
    )(
        right_side.reshape(levels, count, width),
        live_width.reshape(levels),
        lower_source,
        lower_target,
        upper_source,
        upper_target,
        lower_inverse.reshape(levels, width, width),
        upper_inverse.reshape(levels, width, width),
        lower_blocks.reshape(levels, SLOTS, width, width),
        upper_blocks.reshape(levels, SLOTS, width, width),
    )
    forward, backward = pl.pallas_call(
        deliver,
        out_shape=(out, out),
        in_specs=[pl.BlockSpec(memory_space=pltpu.VMEM), pl.BlockSpec(memory_space=pltpu.VMEM)],
        out_specs=(hbm, hbm),
        scratch_shapes=[dma((2, 3))],
        compiler_params=pltpu.CompilerParams(vmem_limit_bytes=1 << 20),
        cost_estimate=pl.CostEstimate(flops=0, bytes_accessed=1 << 20, transcendentals=0),
    )(forward, backward)
    return forward[:, None, None], backward[:, None, None]


def solution(mesh):
    placed = (
        P(None, "prow", "pcol", None, None),
        P(None, "prow", "pcol"),
        P(None, "prow", "pcol", None, None),
        P(None, "prow", "pcol", None, None),
        P(None, "prow", "pcol", None, None, None),
        P(None, "prow", "pcol", None),
        P(None, "prow", "pcol", None),
        P(None, "prow", "pcol", None, None, None),
        P(None, "prow", "pcol", None),
        P(None, "prow", "pcol", None),
    )
    return jax.shard_map(
        functools.partial(local, mesh.shape["pcol"] // NX, mesh.shape["prow"] // CORES),
        mesh=mesh,
        in_specs=placed,
        out_specs=(P(None, "prow", "pcol", None, None), P(None, "prow", "pcol", None, None)),
        check_vma=False,
    )
```

```python
import functools

import jax
import jax.numpy as jnp
from jax import lax
from jax.experimental import pallas as pl
from jax.experimental.pallas import tpu as pltpu
from jax.sharding import PartitionSpec as P


MESH = pl.DeviceIdType.MESH
NX = 4
CORES = 2
CHUNKS = 4
PART = 8
ROWS = CORES * PART
LANES = 128
SLOTS = 4
BF16 = jnp.bfloat16
F32 = jnp.float32
LOW_SOURCE, LOW_TARGET, UP_SOURCE, UP_TARGET, LIVE = 0, 12, 24, 36, 48


def kernel(
    ny,
    nz,
    rhs,
    live_width,
    low_source,
    low_target,
    up_source,
    up_target,
    inv_low,
    inv_up,
    blk_low,
    blk_up,
    out_f,
    out_b,
    rhs_first,
    rhs_rest,
    w_inv_low,
    w_inv_up,
    w_low,
    w_up,
    x_first,
    xf,
    yb,
    piece,
    held,
    stage,
    pick,
    prod,
    acc,
    mine_sum,
    part,
    landed,
    tabs,
    stab,
    local_sem,
    pair_send,
    pair_recv,
    tab_send,
    tab_recv,
    tab_local,
    spread_send,
    spread_recv,
    pick_send,
    pick_recv,
    sum_send,
    sum_recv,
    out_local,
    out_send,
    out_recv,
):
    prow, pcol = lax.axis_index("prow"), lax.axis_index("pcol")
    z, c = prow // CORES, prow % CORES
    y, x = pcol // NX, pcol % NX
    other = 1 - c

    def at(zz, cc, yy, xx):
        return {"prow": zz * CORES + cc, "pcol": yy * NX + xx}

    def remote(src, dst, send, recv, where):
        return pltpu.make_async_remote_copy(
            src_ref=src, dst_ref=dst, send_sem=send, recv_sem=recv, device_id=where, device_id_type=MESH
        )

    partner = at(z, other, y, x)
    mine = pl.ds(pl.multiple_of(c * CHUNKS * PART, CHUNKS * PART), CHUNKS * PART)
    theirs = pl.ds(pl.multiple_of(other * CHUNKS * PART, CHUNKS * PART), CHUNKS * PART)

    barrier = pltpu.get_barrier_semaphore()

    def hello(where):
        pl.semaphore_signal(barrier, inc=1, device_id=where, device_id_type=MESH)

    def far(index, count):
        step = (index + 1) // 2
        return count // 2 + step * (1 - 2 * (index % 2))

    def ring(act, count):
        def one(i, carry):
            act(far(i, count))
            return carry

        lax.fori_loop(0, count - 1, one, 0)

    ring(lambda d: hello(at(z, c, lax.rem(y + d, ny), x)), ny)
    ring(lambda d: hello(at(lax.rem(z + d, nz), c, y, x)), nz)
    for dx in range(1, NX):
        hello(at(z, c, y, lax.rem(x + dx, NX)))
    for dx in range(NX):
        hello(at(z, other, y, lax.rem(x + dx, NX)))

    first_rhs = pltpu.make_async_copy(rhs.at[0], rhs_first, local_sem.at[0])
    first_inv = pltpu.make_async_copy(inv_low.at[0], w_inv_low.at[0, 0], local_sem.at[1])
    first_rhs.start()
    first_inv.start()
    own = []
    shared = []

    def both(src, dst_own, dst_partner, src_partner=None):
        n = len(own)
        own.append(pltpu.make_async_copy(src, dst_own, local_sem.at[2 + n]))
        own[-1].start()
        shared.append(
            remote(src if src_partner is None else src_partner, dst_partner, pair_send.at[1 + n], pair_recv.at[1 + n], partner)
        )
        return n

    got = {}
    got["low", 0] = both(blk_low.at[0], w_low.at[0, 0], w_low.at[0, 1])
    got["low", 1] = both(blk_low.at[1], w_low.at[1, 0], w_low.at[1, 1])
    got["rhs"] = both(rhs.at[pl.ds(1, 2), mine], rhs_rest.at[0], rhs_rest.at[1], rhs.at[pl.ds(1, 2), theirs])
    got["inv_low"] = both(inv_low.at[pl.ds(1, 2)], w_inv_low.at[pl.ds(1, 2), 0], w_inv_low.at[pl.ds(1, 2), 1])
    got["low", 2] = both(blk_low.at[2], w_low.at[2, 0], w_low.at[2, 1])
    got["inv_up"] = both(inv_up, w_inv_up.at[:, 0], w_inv_up.at[:, 1])
    got["up", 2] = both(blk_up.at[2], w_up.at[2, 0], w_up.at[2, 1])
    got["up", 1] = both(blk_up.at[1], w_up.at[1, 0], w_up.at[1, 1])
    got["up", 0] = both(blk_up.at[0], w_up.at[0, 0], w_up.at[0, 1])

    spot = lax.broadcasted_iota(jnp.int32, (8, LANES), 1)
    row = jnp.zeros((8, LANES), jnp.int32)
    for base, small in ((LOW_SOURCE, low_source), (LOW_TARGET, low_target), (UP_SOURCE, up_source), (UP_TARGET, up_target)):
        for pair in range(3):
            for k in range(SLOTS):
                row = jnp.where(spot == base + SLOTS * pair + k, small[pair, 0, 0, k], row)
    for level in range(3):
        row = jnp.where(spot == LIVE + level, live_width[level], row)
    tabs[0, x] = row

    def need(name):
        own[got[name]].wait()
        shared[got[name]].wait_recv()

    lane = lax.broadcasted_iota(jnp.int32, (1, 2 * LANES), 1)

    def live_mask(width):
        return (lane < width).astype(F32)

    def dot(left, right):
        return jnp.dot(left, right, preferred_element_type=F32)

    first_rhs.wait()
    first_inv.wait()
    x_first[...] = live_mask(live_width[0]) * dot(rhs_first[...].astype(BF16), w_inv_low[0, 0])
    xf[0, 0] = x_first[mine, :]
    first_out = pltpu.make_async_copy(x_first, out_f.at[0], out_local.at[0])
    first_out.start()

    pl.semaphore_wait(barrier, (ny - 1) + (nz - 1) + (NX - 1) + NX)
    first_x = remote(x_first.at[theirs], xf.at[0, 1], pair_send.at[0], pair_recv.at[0], partner)
    first_x.start()

    tab_copies = []
    for a in range(CORES):
        for dx in range(NX):
            if (a, dx) != (0, 0):
                tab_copies.append(
                    remote(
                        tabs.at[0, x],
                        tabs.at[a, x],
                        tab_send.at[len(tab_copies)],
                        tab_recv.at[len(tab_copies)],
                        at(z, c if a == 0 else other, y, lax.rem(x + dx, NX)),
                    )
                )
                tab_copies[-1].start()
    for copy in shared[:2]:
        copy.start()

    def halves(own_rows, partner_rows):
        return jnp.concatenate([own_rows, partner_rows], axis=0)

    def rows(r):
        return slice(r * PART, (r + 1) * PART)

    def chunk(ref, r, *place):
        return halves(ref[(0, *place, rows(r))], ref[(1, *place, rows(r))])

    def spread(t, r, tile):
        piece[t, r] = tile.astype(BF16)
        for i in range(ny - 1):
            remote(
                piece.at[t, r],
                held[CHUNKS * t + r].at[y],
                spread_send.at[t, r],
                spread_recv.at[t, r],
                at(z, c, lax.rem(y + far(i, ny), ny), x),
            ).start()
        held[CHUNKS * t + r][y] = tile.astype(BF16)

    def spread_all(t, r):
        span = held[CHUNKS * t + r].at[pl.ds(0, ny - 1)]
        return remote(span, span, spread_send.at[t, r], spread_recv.at[t, r], partner)

    def choose(t, r, n, base):
        have = held[CHUNKS * t + r]
        for d in (2, 1, 3, 0):
            xx = lax.rem(x + d, NX)
            for k in range(SLOTS):
                top, low = [have[lax.div(stab[a, xx, 0, base + k], NX)].astype(F32) for a in range(CORES)]
                tile = halves(top[:PART], low[PART:]).astype(BF16)
                if d:
                    stage[t, r, n, d - 1, k] = tile
                else:
                    pick[(CHUNKS * t + r) * 2 + n][x, k] = tile
            if d:
                remote(
                    stage.at[t, r, n, d - 1],
                    pick[(CHUNKS * t + r) * 2 + n].at[x],
                    pick_send.at[t, r, n],
                    pick_recv.at[t, r, n],
                    at(z, c, y, xx),
                ).start()

    def choose_all(t, r, n):
        span = pick[(CHUNKS * t + r) * 2 + n].at[pl.ds(0, NX - 1)]
        return remote(span, span, pick_send.at[t, r, n], pick_recv.at[t, r, n], partner)

    def products(t, r, n, weights, pair, base):
        choose_all(t, r, n).wait_recv()
        for a in range(CORES):
            for k in range(SLOTS):
                column = lax.rem(stab[a, x, 0, base + k], NX)
                left = pick[(CHUNKS * t + r) * 2 + n][column, k]
                prod[a * SLOTS + k] = dot(left, weights[pair, a, k])[a * PART : (a + 1) * PART]

    def placed(base, d):
        zz = CORES * lax.rem(z + d, nz)
        totals = []
        for to, q in enumerate((zz + c, zz + other)):
            total = None
            for a in range(CORES):
                for k in range(SLOTS):
                    hit = jnp.where(stab[a, x, 0, base + k] == q, 1.0, 0.0).astype(F32)
                    term = prod[a * SLOTS + k] * hit
                    total = term if total is None else total + term
            totals.append(total)
        return halves(*totals)

    def keep(r, base):
        def one(d, carry):
            acc[r, d] = placed(base, d)
            return carry

        lax.fori_loop(0, nz, one, 0)

    def exchange(t, r, base, with_kept):
        def value(d):
            return placed(base, d) + acc[r, d] if with_kept else placed(base, d)

        def send(d):
            part[t, r, d - 1] = value(d).astype(BF16)
            remote(
                part.at[t, r, d - 1],
                landed.at[t, r, d - 1],
                sum_send.at[t, r],
                sum_recv.at[t, r],
                at(lax.rem(z + d, nz), c, y, x),
            ).start()

        ring(send, nz)
        mine_sum[r] = value(0)

    def sum_all(t, r):
        return remote(landed.at[t, r], landed.at[t, r], sum_send.at[t, r], sum_recv.at[t, r], partner)

    def summed(t, r):
        sum_all(t, r).wait_recv()
        total = mine_sum[r]
        for d in range(nz - 1):
            total = total + landed[t, r, d].astype(F32)
        return total

    in_own = lax.broadcasted_iota(jnp.int32, (ROWS, 2 * LANES), 0) < PART
    in_lane = lax.broadcasted_iota(jnp.int32, (ROWS, 2 * LANES), 1)

    def solve(level, weights, residual):
        residual = residual.astype(BF16)
        top, low = [dot(residual, weights[level, a]) for a in range(CORES)]
        width = jnp.where(in_own, stab[0, x, 0, LIVE + level], stab[1, x, 0, LIVE + level])
        return (in_lane < width).astype(F32) * halves(top[:PART], low[PART:])

    def store(ref, level, r, tile):
        for a in range(CORES):
            ref[level, a, rows(r)] = tile[a * PART : (a + 1) * PART]

    out_copies = []

    def put(where, own_rows, partner_rows):
        n = len(out_copies) // 2
        out_copies.append(pltpu.make_async_copy(own_rows, where, out_local.at[1 + n]))
        out_copies.append(remote(partner_rows, where, out_send.at[n], out_recv.at[n], partner))
        out_copies[-2].start()
        out_copies[-1].start()

    def put_level(out, values, level):
        put(out.at[level, mine], values.at[level, 0], values.at[level, 1])

    chunks = range(CHUNKS)

    first_x.wait_recv()
    for r in chunks:
        spread(0, r, chunk(xf.at[0], r))
    for copy in shared[2:]:
        copy.start()
    for copy in tab_copies:
        copy.wait_recv()
    to_scalar = pltpu.make_async_copy(tabs, stab, tab_local)
    to_scalar.start()
    to_scalar.wait()

    def gather(t, base, crit):
        for r in chunks:
            spread_all(t, r).wait_recv()
            choose(t, r, 0, base + SLOTS * crit)

    def multiply(t, weights, name, source, target, crit, late):
        need((name, crit))
        for r in chunks:
            products(t, r, 0, weights, crit, source + SLOTS * crit)
            exchange(t, r, target + SLOTS * crit, late is None)
            if late is not None:
                choose(t, r, 1, source + SLOTS * late)

    def multiply_late(t, r, weights, name, source, target, late):
        if r == 0:
            need((name, late))
        products(t, r, 1, weights, late, source + SLOTS * late)
        keep(r, target + SLOTS * late)

    gather(0, LOW_SOURCE, 0)
    multiply(0, w_low, "low", LOW_SOURCE, LOW_TARGET, 0, 1)
    need("rhs")
    need("inv_low")
    for r in chunks:
        solved = solve(1, w_inv_low, chunk(rhs_rest, r, 0) - summed(0, r))
        spread(1, r, solved)
        store(xf, 1, r, solved)
        multiply_late(0, r, w_low, "low", LOW_SOURCE, LOW_TARGET, 1)
    put_level(out_f, xf, 1)

    gather(1, LOW_SOURCE, 2)
    multiply(1, w_low, "low", LOW_SOURCE, LOW_TARGET, 2, None)
    need("inv_up")
    for r in chunks:
        solved = solve(2, w_inv_low, chunk(rhs_rest, r, 1) - summed(1, r))
        back = solve(2, w_inv_up, solved)
        spread(2, r, back)
        store(xf, 2, r, solved)
        store(yb, 2, r, back)
    put_level(out_f, xf, 2)
    put_level(out_b, yb, 2)

    gather(2, UP_SOURCE, 2)
    multiply(2, w_up, "up", UP_SOURCE, UP_TARGET, 2, 1)
    for r in chunks:
        back = solve(1, w_inv_up, chunk(xf.at[1], r) - summed(2, r))
        spread(3, r, back)
        store(yb, 1, r, back)
        multiply_late(2, r, w_up, "up", UP_SOURCE, UP_TARGET, 1)
    put_level(out_b, yb, 1)

    gather(3, UP_SOURCE, 0)
    multiply(3, w_up, "up", UP_SOURCE, UP_TARGET, 0, None)
    for r in chunks:
        store(yb, 0, r, solve(0, w_inv_up, chunk(xf.at[0], r) - summed(3, r)))
        there = pl.ds(pl.multiple_of(c * CHUNKS * PART + r * PART, PART), PART)
        put(out_b.at[0, there], yb.at[0, 0, pl.ds(r * PART, PART)], yb.at[0, 1, pl.ds(r * PART, PART)])

    first_out.wait()
    first_x.wait_send()
    for copy in shared + tab_copies:
        copy.wait_send()
    for t in range(4):
        for r in chunks:
            spread_all(t, r).wait_send()
            choose_all(t, r, 0).wait_send()
            if t % 2 == 0:
                choose_all(t, r, 1).wait_send()
            sum_all(t, r).wait_send()
    for copy in out_copies:
        copy.wait()


def deliver(forward, backward, out_f, out_b, sem):
    copies = [
        pltpu.make_async_copy(src.at[level], dst.at[level], sem.at[n, level])
        for n, (src, dst) in enumerate(((forward, out_f), (backward, out_b)))
        for level in range(3)
    ]
    for copy in copies:
        copy.start()
    for copy in copies:
        copy.wait()


def local(
    ny,
    nz,
    right_side,
    live_width,
    lower_inverse,
    upper_inverse,
    lower_blocks,
    lower_source,
    lower_target,
    upper_blocks,
    upper_source,
    upper_target,
):
    levels, _, _, count, width = right_side.shape
    dma = pltpu.SemaphoreType.DMA
    hbm = pl.BlockSpec(memory_space=pl.ANY)
    out = jax.ShapeDtypeStruct((levels, count, width), F32)
    forward, backward = pl.pallas_call(
        functools.partial(kernel, ny, nz),
        out_shape=(pltpu.VMEM(out.shape, F32), pltpu.VMEM(out.shape, F32)),
        in_specs=[hbm] + [pl.BlockSpec(memory_space=pltpu.SMEM)] * 5 + [hbm] * 4,
        out_specs=(hbm, hbm),
        scratch_shapes=[
            pltpu.VMEM((count, width), F32),
            pltpu.VMEM((CORES, levels - 1, CHUNKS * PART, width), F32),
            pltpu.VMEM((levels, CORES, width, width), BF16),
            pltpu.VMEM((levels, CORES, width, width), BF16),
            pltpu.VMEM((levels, CORES, SLOTS, width, width), BF16),
            pltpu.VMEM((levels, CORES, SLOTS, width, width), BF16),
            pltpu.VMEM((count, width), F32),
            pltpu.VMEM((levels, CORES, CHUNKS * PART, width), F32),
            pltpu.VMEM((levels, CORES, CHUNKS * PART, width), F32),
            pltpu.VMEM((4, CHUNKS, ROWS, width), BF16),
            [pltpu.VMEM((ny, ROWS, width), BF16) for _ in range(4 * CHUNKS)],
            pltpu.VMEM((4, CHUNKS, 2, NX - 1, SLOTS, ROWS, width), BF16),
            [pltpu.VMEM((NX, SLOTS, ROWS, width), BF16) for _ in range(8 * CHUNKS)],
            pltpu.VMEM((CORES * SLOTS, PART, width), F32),
            pltpu.VMEM((CHUNKS, nz, ROWS, width), F32),
            pltpu.VMEM((CHUNKS, ROWS, width), F32),
            pltpu.VMEM((4, CHUNKS, nz - 1, ROWS, width), BF16),
            pltpu.VMEM((4, CHUNKS, nz - 1, ROWS, width), BF16),
            pltpu.VMEM((CORES, NX, 8, LANES), jnp.int32),
            pltpu.SMEM((CORES, NX, 8, LANES), jnp.int32),
            dma((11,)),
            dma((10,)),
            dma((10,)),
            dma((7,)),
            dma((7,)),
            dma(()),
            dma((4, CHUNKS)),
            dma((4, CHUNKS)),
            dma((4, CHUNKS, 2)),
            dma((4, CHUNKS, 2)),
            dma((4, CHUNKS)),
            dma((4, CHUNKS)),
            dma((5 + CHUNKS,)),
            dma((4 + CHUNKS,)),
            dma((4 + CHUNKS,)),
        ],
        compiler_params=pltpu.CompilerParams(collective_id=0, has_side_effects=True, vmem_limit_bytes=60 << 20),
        cost_estimate=pl.CostEstimate(flops=252 << 20, bytes_accessed=8 << 20, transcendentals=0),
    )(
        right_side.reshape(levels, count, width),
        live_width.reshape(levels),
        lower_source,
        lower_target,
        upper_source,
        upper_target,
        lower_inverse.reshape(levels, width, width),
        upper_inverse.reshape(levels, width, width),
        lower_blocks.reshape(levels, SLOTS, width, width),
        upper_blocks.reshape(levels, SLOTS, width, width),
    )
    forward, backward = pl.pallas_call(
        deliver,
        out_shape=(out, out),
        in_specs=[pl.BlockSpec(memory_space=pltpu.VMEM), pl.BlockSpec(memory_space=pltpu.VMEM)],
        out_specs=(hbm, hbm),
        scratch_shapes=[dma((2, 3))],
        compiler_params=pltpu.CompilerParams(vmem_limit_bytes=1 << 20),
        cost_estimate=pl.CostEstimate(flops=0, bytes_accessed=1 << 20, transcendentals=0),
    )(forward, backward)
    return forward[:, None, None], backward[:, None, None]


def solution(mesh):
    placed = (
        P(None, "prow", "pcol", None, None),
        P(None, "prow", "pcol"),
        P(None, "prow", "pcol", None, None),
        P(None, "prow", "pcol", None, None),
        P(None, "prow", "pcol", None, None, None),
        P(None, "prow", "pcol", None),
        P(None, "prow", "pcol", None),
        P(None, "prow", "pcol", None, None, None),
        P(None, "prow", "pcol", None),
        P(None, "prow", "pcol", None),
    )
    return jax.shard_map(
        functools.partial(local, mesh.shape["pcol"] // NX, mesh.shape["prow"] // CORES),
        mesh=mesh,
        in_specs=placed,
        out_specs=(P(None, "prow", "pcol", None, None), P(None, "prow", "pcol", None, None)),
        check_vma=False,
    )
```
